32 devices in a mesh: seq: 16 (over z, x, core), ch: 2 (over y).
Axes of the slice: x: 2, y: 2, z: 4, core: 2. Of those that a mesh axis runs over, the one named last changes fastest.
Arguments:
- tokens: bfloat16 [2, 65536, 2048], P(None, 'seq', 'ch'), may hold values from -6 to 6
- inner_forward: bfloat16 [512, 512], replicated, may hold values from -0.25 to 0.25
- outer_forward: bfloat16 [128, 128], replicated, may hold values from -0.5 to 0.5
- twiddle_forward: float32 [128, 512], P('seq'), may hold values from 0.5 to 2
- freq_kernel: bfloat16 [128, 512, 2048], P(None, 'seq', 'ch'), may hold values from -6 to 6
- outer_inverse: bfloat16 [128, 128], replicated, may hold values from -0.5 to 0.5
- inner_inverse: bfloat16 [512, 512], replicated, may hold values from -0.25 to 0.25
- twiddle_inverse: float32 [128, 512], P(None, 'seq'), may hold values from 0.5 to 2
- gate_gain: float32 [2048], P('ch'), may hold values from 0.5 to 1.5
- gate_bias: float32 [2048], P('ch'), may hold values from -1 to 1
- norm_gain: float32 [2048], replicated, may hold values from 0.1 to 1.9
- up_weight: bfloat16 [4, 1024, 512], P(None, 'seq'), may hold values from -0.25 to 0.25
- down_weight: bfloat16 [4, 1024, 512], P(None, 'seq'), may hold values from -0.1875 to 0.1875
Outputs:
- layer_out: bfloat16 [2, 65536, 2048], P(None, 'seq', 'ch')
The draws below stay inside these ranges and needn't reach their ends.
All inputs are finite; a program needn't handle non-finite values.
Results may differ from the reference program's by a relative error of at most 0.008.
Values may be sent and summed in bfloat16 or wider, within the bound.
No kernel may reach another device: no remote copies, remote signals or barrier semaphores. Data moves between devices by JAX's collectives and lax.ppermute only.
A program may use at most 256 MiB of HBM per device.

```python
import math
import jax
import jax.numpy as jnp
from jax import lax

NA = 128
NB = 512
D = 2048
H = 4096
BLOCKS = 4
BATCH = 2
SEQ_LEN = 65536


def shard_levels(stream_key, shape, split, smallest, top_value):
    def one(dim, shards_of):
        draws = jax.random.uniform(jax.random.fold_in(jax.random.fold_in(stream_key, 6), dim), (shards_of,), jnp.float32, smallest / len(split), top_value / len(split))
        return jnp.repeat(jnp.exp(draws), shape[dim] // shards_of).reshape((-1,) + (1,) * (len(shape) - dim - 1))

    factor_of = one(*split[0])
    for cut in split[1:]:
        factor_of = factor_of * one(*cut)
    return factor_of


def normal_values(stream_key, dims, spread, most, shards=(), kind=jnp.bfloat16):
    array = spread * jax.random.normal(stream_key, dims, jnp.float32)
    if shards:
        array = array * shard_levels(stream_key, dims, shards, -0.22, 0.18)
    return jnp.clip(array, -most, most).astype(kind)


def setup_inputs(seed: int = 0) -> dict:
    streams_of = jax.random.split(jax.random.key(seed), 14)
    tokens = normal_values(streams_of[0], (BATCH, SEQ_LEN, D), 1.0, 6.0, ((1, 16), (2, 2)))
    inner_forward = normal_values(streams_of[1], (NB, NB), NB ** -0.5, 0.25)
    outer_forward = normal_values(streams_of[2], (NA, NA), NA ** -0.5, 0.5)
    twiddle_forward = jnp.clip(jnp.exp(math.log(2.0) - 1.3862944 * jax.random.uniform(streams_of[3], (NA, NB), jnp.float32) ** shard_levels(streams_of[3], (NA, NB), ((0, 16),), -0.2, 0.2)), 0.5, 2.0)
    freq_kernel = normal_values(streams_of[4], (NA, NB, D), 1.0, 6.0, ((1, 16), (2, 2)))
    outer_inverse = normal_values(streams_of[5], (NA, NA), NA ** -0.5, 0.5)
    inner_inverse = normal_values(streams_of[6], (NB, NB), NB ** -0.5, 0.25)
    twiddle_inverse = jnp.clip(jnp.exp(math.log(2.0) - 1.3862944 * jax.random.uniform(streams_of[7], (NA, NB), jnp.float32) ** shard_levels(streams_of[7], (NA, NB), ((1, 16),), -0.2, 0.2)), 0.5, 2.0)
    gate_gain = jnp.clip(0.5 + 1.0 * jax.random.uniform(streams_of[8], (D,), jnp.float32) ** shard_levels(streams_of[8], (D,), ((0, 2),), -0.2, 0.2), 0.5, 1.5)
    gate_bias = jnp.clip(jax.random.uniform(streams_of[9], (D,), jnp.float32, -1.0, 1.0) * shard_levels(streams_of[9], (D,), ((0, 2),), -0.4, 0.0), -1.0, 1.0)
    norm_gain = jnp.clip(1.0 + 0.18 * jax.random.normal(streams_of[10], (D,), jnp.float32), 0.1, 1.9)
    up_weight = normal_values(streams_of[11], (BLOCKS, H // BLOCKS, D // BLOCKS), (D // BLOCKS) ** -0.5, 0.25, ((1, 16),))
    down_weight = normal_values(streams_of[12], (BLOCKS, H // BLOCKS, D // BLOCKS), (H // BLOCKS) ** -0.5, 0.1875, ((1, 16),))
    return dict(tokens=tokens, inner_forward=inner_forward, outer_forward=outer_forward, twiddle_forward=twiddle_forward, freq_kernel=freq_kernel, outer_inverse=outer_inverse, inner_inverse=inner_inverse, twiddle_inverse=twiddle_inverse, gate_gain=gate_gain, gate_bias=gate_bias, norm_gain=norm_gain, up_weight=up_weight, down_weight=down_weight)


def reference(tokens, inner_forward, outer_forward, twiddle_forward, freq_kernel, outer_inverse, inner_inverse, twiddle_inverse, gate_gain, gate_bias, norm_gain, up_weight, down_weight):
    width_block = D // BLOCKS
    rows_block = min(NA * NB, 4096)

    def one_sequence(sequence):
        grid = sequence.reshape(NA, NB, D).astype(jnp.float32)
        section_one = (jnp.einsum('kb,abc->akc', inner_forward.astype(jnp.float32), grid) * twiddle_forward[:, :, None]).astype(jnp.bfloat16)
        spectrum = (jnp.einsum('ka,abc->kbc', outer_forward.astype(jnp.float32), section_one.astype(jnp.float32)) * freq_kernel.astype(jnp.float32)).astype(jnp.bfloat16)
        section_two = (jnp.einsum('nk,kbc->nbc', outer_inverse.astype(jnp.float32), spectrum.astype(jnp.float32)) * twiddle_inverse[:, :, None]).astype(jnp.bfloat16)
        mixed = jnp.einsum('mk,nkc->nmc', inner_inverse.astype(jnp.float32), section_two.astype(jnp.float32)).reshape(NA * NB, D)
        flat = sequence.astype(jnp.float32)
        gate = jax.nn.sigmoid(flat * gate_gain + gate_bias)
        gated = (flat + gate * mixed).astype(jnp.bfloat16)

        def mlp_block(rows):
            rows_f = rows.astype(jnp.float32)
            scale = lax.rsqrt(lax.optimization_barrier(jnp.mean(rows_f * rows_f, axis=-1, keepdims=True)) + 1e-06)
            normed = (rows_f * scale * norm_gain).astype(jnp.bfloat16)
            normed_b = normed.reshape(-1, BLOCKS, width_block).astype(jnp.float32)
            lifted = jnp.einsum('tbi,bji->tbj', normed_b, up_weight.astype(jnp.float32))
            hidden = jax.nn.gelu(lifted, approximate=True).astype(jnp.bfloat16)
            lowered = jnp.einsum('tbj,bji->tbi', hidden.astype(jnp.float32), down_weight.astype(jnp.float32)).reshape(-1, D)
            return (rows_f + lowered).astype(jnp.bfloat16)
        blocks = gated.reshape(-1, rows_block, D)
        return lax.map(mlp_block, blocks).reshape(NA * NB, D)
    return lax.map(one_sequence, tokens)
```

```python
import functools

import jax
import jax.numpy as jnp
from jax import lax
from jax.experimental import pallas as pl
from jax.experimental.pallas import tpu as pltpu
from jax.sharding import PartitionSpec as P

VMEM_BYTES = 56 * 1024 * 1024
EPS = 1e-06
GROUPS = ((8,), (4, 2, 1, 1))


def params():
    return pltpu.CompilerParams(vmem_limit_bytes=VMEM_BYTES)


def first_kernel(n, me_ref, tok_ref, w_ref, tw_ref, *rest):
    outs, buf = rest[:n], rest[n]
    a = pl.program_id(0)
    res = jnp.dot(w_ref[...], tok_ref[0, 0], preferred_element_type=jnp.float32)
    cols = tw_ref[...].T
    lane = lax.broadcasted_iota(jnp.int32, cols.shape, 1)
    tw = jnp.sum(jnp.where(lane == a, cols, 0.0), axis=1, keepdims=True)
    buf[...] = (res * tw).astype(jnp.bfloat16)
    rows = buf.shape[0] // n
    for m in range(n):
        start = pl.multiple_of((me_ref[0] ^ m) * rows, rows)
        outs[m][0] = buf[pl.ds(start, rows), :]


def first_section(me, blocked, inner_forward, twiddle, s, n):
    _, a_dev, inner, ch = blocked.shape
    rows = inner // n
    return pl.pallas_call(
        functools.partial(first_kernel, n),
        grid_spec=pltpu.PrefetchScalarGridSpec(
            num_scalar_prefetch=1,
            grid=(a_dev,),
            in_specs=[
                pl.BlockSpec((1, 1, inner, ch), lambda a, me: (s, a, 0, 0)),
                pl.BlockSpec((inner, inner), lambda a, me: (0, 0)),
                pl.BlockSpec((a_dev, inner), lambda a, me: (0, 0)),
            ],
            out_specs=[pl.BlockSpec((1, rows, ch), lambda a, me: (a, 0, 0))] * n,
            scratch_shapes=[pltpu.VMEM((inner, ch), jnp.bfloat16)],
        ),
        out_shape=[jax.ShapeDtypeStruct((a_dev, rows, ch), jnp.bfloat16)] * n,
        compiler_params=params(),
        name="first_section",
    )(me, blocked, inner_forward, twiddle)


def gate_kernel(n, me_ref, tok_ref, w_ref, gain_ref, bias_ref, *rest):
    parts, gated_ref, sq_ref, buf = rest[:n], rest[n], rest[n + 1], rest[n + 2]
    rows = buf.shape[0] // n
    for m in range(n):
        start = pl.multiple_of((me_ref[0] ^ m) * rows, rows)
        buf[pl.ds(start, rows), :] = parts[m][0]
    mixed = jnp.dot(w_ref[...], buf[...], preferred_element_type=jnp.float32)
    flat = tok_ref[0, 0].astype(jnp.float32)
    gate = jax.nn.sigmoid(flat * gain_ref[...] + bias_ref[...])
    gated = (flat + gate * mixed).astype(jnp.bfloat16)
    gated_ref[0] = gated
    g = gated.astype(jnp.float32)
    sq = g * g
    part = sq[:, :128]
    for c in range(128, sq.shape[1], 128):
        part = part + sq[:, c : c + 128]
    sq_ref[0] = jnp.sum(part.T, axis=0, keepdims=True)


def gate_rows(me, blocked, inner_inverse, gain, bias, parts, s, first, n):
    _, _, inner, ch = blocked.shape
    count, rows, _ = parts[0].shape
    return pl.pallas_call(
        functools.partial(gate_kernel, n),
        grid_spec=pltpu.PrefetchScalarGridSpec(
            num_scalar_prefetch=1,
            grid=(count,),
            in_specs=[
                pl.BlockSpec((1, 1, inner, ch), lambda j, me: (s, first + j, 0, 0)),
                pl.BlockSpec((inner, inner), lambda j, me: (0, 0)),
                pl.BlockSpec((1, ch), lambda j, me: (0, 0)),
                pl.BlockSpec((1, ch), lambda j, me: (0, 0)),
            ]
            + [pl.BlockSpec((1, rows, ch), lambda j, me: (j, 0, 0))] * n,
            out_specs=[
                pl.BlockSpec((1, inner, ch), lambda j, me: (j, 0, 0)),
                pl.BlockSpec((1, 1, inner), lambda j, me: (j, 0, 0)),
            ],
            scratch_shapes=[pltpu.VMEM((inner, ch), jnp.bfloat16)],
        ),
        out_shape=[
            jax.ShapeDtypeStruct((count, inner, ch), jnp.bfloat16),
            jax.ShapeDtypeStruct((count, 1, inner), jnp.float32),
        ],
        compiler_params=params(),
        name="gate_rows",
    )(me, blocked, inner_inverse, gain, bias, *parts)


def mlp_kernel(width, gated_ref, sq_ref, gain_ref, up_ref, down_ref, *rest):
    out_ref = rest[-1]
    blocks, _, wb = up_ref.shape
    scale = lax.rsqrt(sq_ref[0] * (1.0 / width) + EPS)
    scale = jnp.broadcast_to(scale, (128, scale.shape[1])).T[:, :1]
    for b in range(blocks):
        cols = slice(b * wb, (b + 1) * wb)
        g = gated_ref[0, :, cols].astype(jnp.float32)
        normed = (g * scale * gain_ref[:, cols]).astype(jnp.bfloat16)
        lifted = lax.dot_general(
            normed, up_ref[b], (((1,), (1,)), ((), ())), preferred_element_type=jnp.float32
        )
        hidden = jax.nn.gelu(lifted, approximate=True).astype(jnp.bfloat16)
        lowered = jnp.dot(hidden, down_ref[b], preferred_element_type=jnp.float32)
        out_ref[0, :, cols] = (g + lowered).astype(jnp.bfloat16)


def mlp_rows(gated, sq, gain, up, down, out, first, total, width):
    count, inner, ch = gated.shape
    specs = [
        pl.BlockSpec((1, inner, ch), lambda j: (j, 0, 0)),
        pl.BlockSpec((1, 1, inner), lambda j: (j, 0, 0)),
        pl.BlockSpec((1, ch), lambda j: (0, 0)),
        pl.BlockSpec(up.shape, lambda j: (0, 0, 0), pipeline_mode=pl.Buffered(1)),
        pl.BlockSpec(down.shape, lambda j: (0, 0, 0), pipeline_mode=pl.Buffered(1)),
    ]
    args = [gated, sq, gain, up, down]
    aliases = {}
    if out is not None:
        specs.append(pl.BlockSpec(memory_space=pl.ANY))
        args.append(out)
        aliases = {5: 0}
    return pl.pallas_call(
        functools.partial(mlp_kernel, width),
        grid=(count,),
        in_specs=specs,
        out_specs=pl.BlockSpec((1, inner, ch), lambda j: (first + j, 0, 0)),
        out_shape=jax.ShapeDtypeStruct((total, inner, ch), jnp.bfloat16),
        input_output_aliases=aliases,
        compiler_params=params(),
        name="mlp_rows",
    )(*args)


def swap(x, m, n):
    return lax.ppermute(x, "seq", [(j, j ^ m) for j in range(n)])


def send_order(n):
    half = n // 2
    order = []
    for j in range(half):
        order.append(half + j)
        if j:
            order.append(j)
    return order


def exchange(parts, n):
    got = list(parts)
    for m in send_order(n):
        got[m] = swap(parts[m], m, n)
    return got


def local_blocks(
    tokens,
    inner_forward,
    outer_forward,
    twiddle_forward,
    freq_kernel,
    outer_inverse,
    inner_inverse,
    twiddle_inverse,
    gate_gain,
    gate_bias,
    norm_gain,
    up_weight,
    down_weight,
):
    seqs, tok_dev, ch = tokens.shape
    inner = inner_forward.shape[0]
    a_dev = tok_dev // inner
    n = lax.axis_size("seq")
    n_ch = lax.axis_size("ch")
    me = lax.axis_index("seq")
    my_ch = lax.axis_index("ch")
    outer = n * a_dev
    me_arr = jnp.reshape(me, (1,)).astype(jnp.int32)
    blocked = tokens.reshape(seqs, a_dev, inner, ch)
    order = jnp.arange(n) ^ me
    forward = outer_forward.reshape(outer, n, a_dev)[:, order].reshape(outer, outer)
    inverse = outer_inverse.reshape(n, a_dev, outer)[order].reshape(outer, outer)
    tw_inv = twiddle_inverse.reshape(n, a_dev, -1)[order].reshape(outer, -1)

    held = ch // up_weight.shape[2]
    up = lax.dynamic_slice_in_dim(up_weight, my_ch * held, held, 0)
    down = lax.dynamic_slice_in_dim(down_weight, my_ch * held, held, 0)
    up = lax.all_gather(up, "seq", axis=1, tiled=True)
    down = lax.all_gather(down, "seq", axis=1, tiled=True)
    norm = lax.dynamic_slice_in_dim(norm_gain, my_ch * ch, ch, 0).reshape(1, ch)
    gain, bias = gate_gain.reshape(1, ch), gate_bias.reshape(1, ch)

    got = []
    for s in range(seqs):
        parts = first_section(me_arr, blocked, inner_forward, twiddle_forward, s, n)
        got.append(exchange(parts, n))

    out = None
    for s in range(seqs):
        spread = jnp.concatenate(got[s], axis=0)
        spectrum = jnp.einsum("ka,abc->kbc", forward, spread, preferred_element_type=jnp.float32)
        spectrum = (spectrum * freq_kernel.astype(jnp.float32)).astype(jnp.bfloat16)
        section_two = jnp.einsum(
            "nk,kbc->nbc", inverse, spectrum, preferred_element_type=jnp.float32
        )
        section_two = (section_two * tw_inv[:, :, None]).astype(jnp.bfloat16)
        section_two = section_two.reshape(n, a_dev, -1, ch)
        first = 0
        for count in GROUPS[min(s, 1)]:
            parts = [section_two[m, first : first + count] for m in range(n)]
            parts = exchange(parts, n)
            gated, sq = gate_rows(
                me_arr, blocked, inner_inverse, gain, bias, parts, s, first, n
            )
            total = sq
            for r in range(1, n_ch):
                total = total + lax.ppermute(
                    sq, "ch", [(j, (j + r) % n_ch) for j in range(n_ch)]
                )
            out = mlp_rows(
                gated, total, norm, up, down, out, s * a_dev + first, seqs * a_dev, ch * n_ch
            )
            first += count
    return out.reshape(seqs, tok_dev, ch)


def local_rows(
    tokens,
    inner_forward,
    outer_forward,
    twiddle_forward,
    freq_kernel,
    outer_inverse,
    inner_inverse,
    twiddle_inverse,
    gate_gain,
    gate_bias,
    norm_gain,
    up_weight,
    down_weight,
):
    seq_total, tok_dev, ch_dev = tokens.shape
    inner_size = inner_forward.shape[0]
    outer_dev = tok_dev // inner_size
    blocked = tokens.reshape(seq_total, outer_dev, inner_size, ch_dev)
    section_one = jnp.einsum(
        "kb,xabc->xakc", inner_forward, blocked, preferred_element_type=jnp.float32
    )
    section_one = (section_one * twiddle_forward[None, :, :, None]).astype(jnp.bfloat16)
    spread = lax.all_to_all(section_one, "seq", split_axis=2, concat_axis=1, tiled=True)
    spectrum = jnp.einsum(
        "ka,xabc->xkbc", outer_forward, spread, preferred_element_type=jnp.float32
    )
    spectrum = (spectrum * freq_kernel[None].astype(jnp.float32)).astype(jnp.bfloat16)
    section_two = jnp.einsum(
        "nk,xkbc->xnbc", outer_inverse, spectrum, preferred_element_type=jnp.float32
    )
    section_two = (section_two * twiddle_inverse[None, :, :, None]).astype(jnp.bfloat16)
    gathered = lax.all_to_all(section_two, "seq", split_axis=1, concat_axis=2, tiled=True)
    block_count = up_weight.shape[0]
    width_block = up_weight.shape[2]
    mixed = jnp.einsum("mk,xakc->xamc", inner_inverse, gathered, preferred_element_type=jnp.float32)
    flat = blocked.astype(jnp.float32)
    gate = jax.nn.sigmoid(flat * gate_gain + gate_bias)
    gated = (flat + gate * mixed).astype(jnp.bfloat16)
    full_rows = lax.all_to_all(
        gated.reshape(blocked.shape[0], tok_dev, ch_dev),
        "ch",
        split_axis=1,
        concat_axis=2,
        tiled=True,
    )
    rows_dev = full_rows.shape[1]
    width = full_rows.shape[2]
    rows_f = full_rows.astype(jnp.float32)
    scale = lax.rsqrt(jnp.mean(rows_f * rows_f, axis=-1, keepdims=True) + EPS)
    normed = (rows_f * scale * norm_gain).astype(jnp.bfloat16)
    normed_b = normed.reshape(seq_total * rows_dev, block_count, width_block)
    lifted = jnp.einsum(
        "rbi,bji->rbj",
        normed_b,
        lax.all_gather(up_weight, "seq", axis=1, tiled=True),
        preferred_element_type=jnp.float32,
    )
    hidden = jax.nn.gelu(lifted, approximate=True).astype(jnp.bfloat16)
    lowered = jnp.einsum(
        "rbj,bji->rbi",
        hidden,
        lax.all_gather(down_weight, "seq", axis=1, tiled=True),
        preferred_element_type=jnp.float32,
    )
    result_rows = (rows_f + lowered.reshape(seq_total, rows_dev, width)).astype(jnp.bfloat16)
    return lax.all_to_all(result_rows, "ch", split_axis=2, concat_axis=1, tiled=True)


def local(*args):
    tokens, up_weight = args[0], args[11]
    n = lax.axis_size("seq")
    if tokens.shape[2] % up_weight.shape[2] == 0 and n & (n - 1) == 0:
        return local_blocks(*args)
    return local_rows(*args)


def solution(mesh):
    in_specs = (
        P(None, "seq", "ch"),
        P(),
        P(),
        P("seq", None),
        P(None, "seq", "ch"),
        P(),
        P(),
        P(None, "seq"),
        P("ch"),
        P("ch"),
        P(),
        P(None, "seq", None),
        P(None, "seq", None),
    )
    out_specs = P(None, "seq", "ch")
    return jax.shard_map(local, mesh=mesh, in_specs=in_specs, out_specs=out_specs, check_vma=False)
```

```python
import functools

import jax
import jax.numpy as jnp
from jax import lax
from jax.experimental import pallas as pl
from jax.experimental.pallas import tpu as pltpu
from jax.sharding import PartitionSpec as P

VMEM_BYTES = 56 * 1024 * 1024
EPS = 1e-06
RETURN_ROWS = ((8,), (6, 2))
GATE_ROWS = 4
MLP_ROWS = 4


def params():
    return pltpu.CompilerParams(vmem_limit_bytes=VMEM_BYTES)


def first_kernel(tok_ref, w_ref, tw_ref, out_ref):
    a = pl.program_id(0)
    res = jnp.dot(w_ref[...], tok_ref[0, 0], preferred_element_type=jnp.float32)
    cols = tw_ref[...].T
    lane = lax.broadcasted_iota(jnp.int32, cols.shape, 1)
    tw = jnp.sum(jnp.where(lane == a, cols, 0.0), axis=1, keepdims=True)
    n, _, rows, ch = out_ref.shape
    out_ref[...] = (res * tw).astype(jnp.bfloat16).reshape(n, 1, rows, ch)


def first_section(blocked, inner_forward, twiddle, s, n):
    _, a_dev, inner, ch = blocked.shape
    rows = inner // n
    return pl.pallas_call(
        first_kernel,
        grid=(a_dev,),
        in_specs=[
            pl.BlockSpec((1, 1, inner, ch), lambda a: (s, a, 0, 0)),
            pl.BlockSpec((inner, inner), lambda a: (0, 0)),
            pl.BlockSpec((a_dev, inner), lambda a: (0, 0)),
        ],
        out_specs=pl.BlockSpec((n, 1, rows, ch), lambda a: (0, a, 0, 0)),
        out_shape=jax.ShapeDtypeStruct((n, a_dev, rows, ch), jnp.bfloat16),
        compiler_params=params(),
        name="first_section",
    )(blocked, inner_forward, twiddle)


def outer_kernel(groups, fwd_ref, inv_ref, tw_ref, freq_ref, spread_ref, *rest):
    outs, (xs, fs, ys) = rest[:-3], rest[-3:]
    steps, outer, block = xs.shape
    xs[...] = jnp.swapaxes(spread_ref[...].astype(jnp.float32), 0, 1)
    fs[...] = jnp.swapaxes(freq_ref[...].astype(jnp.float32), 0, 1)
    tw = tw_ref[0]
    for k in range(steps):
        spectrum = jnp.dot(
            fwd_ref[...], xs[k].astype(jnp.bfloat16), preferred_element_type=jnp.float32
        )
        spectrum = (spectrum * fs[k]).astype(jnp.bfloat16)
        two = jnp.dot(inv_ref[...], spectrum, preferred_element_type=jnp.float32)
        ys[k] = two * tw[:, k : k + 1]
    res = jnp.swapaxes(ys[...], 0, 1).astype(jnp.bfloat16)
    n = outs[0].shape[0]
    res = res.reshape(n, outer // n, steps, block)
    first = 0
    for out, count in zip(outs, groups):
        out[...] = res[:, first : first + count]
        first += count


def outer_section(spread, forward, inverse, tw, freq, groups, n):
    outer, k_dev, ch = freq.shape
    rows, block = min(16, k_dev), min(256, ch)
    tw = tw.reshape(outer, k_dev // rows, rows).swapaxes(0, 1)
    return pl.pallas_call(
        functools.partial(outer_kernel, groups),
        grid=(k_dev // rows, ch // block),
        in_specs=[
            pl.BlockSpec((outer, outer), lambda h, c: (0, 0)),
            pl.BlockSpec((outer, outer), lambda h, c: (0, 0)),
            pl.BlockSpec((1, outer, rows), lambda h, c: (h, 0, 0)),
            pl.BlockSpec((outer, rows, block), lambda h, c: (0, h, c)),
            pl.BlockSpec((outer, rows, block), lambda h, c: (0, h, c)),
        ],
        out_specs=[
            pl.BlockSpec((n, count, rows, block), lambda h, c: (0, 0, h, c)) for count in groups
        ],
        out_shape=[
            jax.ShapeDtypeStruct((n, count, k_dev, ch), jnp.bfloat16) for count in groups
        ],
        scratch_shapes=[pltpu.VMEM((rows, outer, block), jnp.float32)] * 3,
        compiler_params=params(),
        name="outer_section",
    )(forward, inverse, tw, freq, spread)


def gate_kernel(tok_ref, w_ref, gain_ref, bias_ref, part_ref, gated_ref, sq_ref):
    flat = tok_ref[0, 0].astype(jnp.float32)
    section = part_ref[...].reshape(flat.shape)
    mixed = jnp.dot(w_ref[...], section, preferred_element_type=jnp.float32)
    gate = jax.nn.sigmoid(flat * gain_ref[...] + bias_ref[...])
    gated = (flat + gate * mixed).astype(jnp.bfloat16)
    gated_ref[0] = gated
    g = gated.astype(jnp.float32)
    sq = g * g
    part = sq[:, :128]
    for c in range(128, sq.shape[1], 128):
        part = part + sq[:, c : c + 128]
    sq_ref[0] = jnp.sum(part.T, axis=0, keepdims=True)


def gate_rows(blocked, inner_inverse, gain, bias, parts, s, first, skip, count):
    _, _, inner, ch = blocked.shape
    n, _, rows, _ = parts.shape
    return pl.pallas_call(
        gate_kernel,
        grid=(count,),
        in_specs=[
            pl.BlockSpec((1, 1, inner, ch), lambda j: (s, first + skip + j, 0, 0)),
            pl.BlockSpec((inner, inner), lambda j: (0, 0)),
            pl.BlockSpec((1, ch), lambda j: (0, 0)),
            pl.BlockSpec((1, ch), lambda j: (0, 0)),
            pl.BlockSpec((n, 1, rows, ch), lambda j: (0, skip + j, 0, 0)),
        ],
        out_specs=[
            pl.BlockSpec((1, inner, ch), lambda j: (j, 0, 0)),
            pl.BlockSpec((1, 1, inner), lambda j: (j, 0, 0)),
        ],
        out_shape=[
            jax.ShapeDtypeStruct((count, inner, ch), jnp.bfloat16),
            jax.ShapeDtypeStruct((count, 1, inner), jnp.float32),
        ],
        compiler_params=params(),
        name="gate_rows",
    )(blocked, inner_inverse, gain, bias, parts)


def mlp_kernel(width, gated_ref, sq_ref, gain_ref, weight_ref, *rest):
    out_ref = rest[-1]
    _, blocks, _, wb = weight_ref.shape
    scale = lax.rsqrt(sq_ref[0] * (1.0 / width) + EPS)
    scale = jnp.broadcast_to(scale, (128, scale.shape[1])).T[:, :1]
    for b in range(blocks):
        cols = slice(b * wb, (b + 1) * wb)
        g = gated_ref[0, :, cols].astype(jnp.float32)
        normed = (g * scale * gain_ref[:, cols]).astype(jnp.bfloat16)
        lifted = lax.dot_general(
            normed, weight_ref[0, b], (((1,), (1,)), ((), ())), preferred_element_type=jnp.float32
        )
        hidden = jax.nn.gelu(lifted, approximate=True).astype(jnp.bfloat16)
        lowered = jnp.dot(hidden, weight_ref[1, b], preferred_element_type=jnp.float32)
        out_ref[0, :, cols] = (g + lowered).astype(jnp.bfloat16)


def mlp_rows(gated, sq, gain, weights, out, skip, count, first, total, width):
    _, inner, ch = gated.shape
    specs = [
        pl.BlockSpec((1, inner, ch), lambda j: (skip + j, 0, 0)),
        pl.BlockSpec((1, 1, inner), lambda j: (skip + j, 0, 0)),
        pl.BlockSpec((1, ch), lambda j: (0, 0)),
        pl.BlockSpec(weights.shape, lambda j: (0, 0, 0, 0), pipeline_mode=pl.Buffered(1)),
    ]
    args = [gated, sq, gain, weights]
    aliases = {}
    if out is not None:
        specs.append(pl.BlockSpec(memory_space=pl.ANY))
        args.append(out)
        aliases = {4: 0}
    return pl.pallas_call(
        functools.partial(mlp_kernel, width),
        grid=(count,),
        in_specs=specs,
        out_specs=pl.BlockSpec((1, inner, ch), lambda j: (first + j, 0, 0)),
        out_shape=jax.ShapeDtypeStruct((total, inner, ch), jnp.bfloat16),
        input_output_aliases=aliases,
        compiler_params=params(),
        name="mlp_rows",
    )(*args)


def after(x, *deps):
    return lax.optimization_barrier((x,) + deps)[0]


def after(x, *deps):
    return lax.optimization_barrier((x,) + deps)[0]


def exchange(x):
    return lax.all_to_all(x, "seq", split_axis=0, concat_axis=0, tiled=True)


def more_hidden(weights, n, step):
    other = lax.ppermute(weights, "seq", [(j, j ^ step) for j in range(n)])
    return jnp.concatenate([weights, other], axis=2)


def local_blocks(
    tokens,
    inner_forward,
    outer_forward,
    twiddle_forward,
    freq_kernel,
    outer_inverse,
    inner_inverse,
    twiddle_inverse,
    gate_gain,
    gate_bias,
    norm_gain,
    up_weight,
    down_weight,
):

    seqs, tok_dev, ch = tokens.shape
    inner = inner_forward.shape[0]
    a_dev = tok_dev // inner
    n = lax.axis_size("seq")
    n_ch = lax.axis_size("ch")
    my_ch = lax.axis_index("ch")
    outer = n * a_dev
    blocked = tokens.reshape(seqs, a_dev, inner, ch)
    norm = lax.dynamic_slice_in_dim(norm_gain, my_ch * ch, ch, 0).reshape(1, ch)
    gain, bias = gate_gain.reshape(1, ch), gate_bias.reshape(1, ch)
    held = ch // up_weight.shape[2]
    weights = lax.dynamic_slice_in_dim(
        jnp.stack([up_weight, down_weight]), my_ch * held, held, 1
    )
    weights = more_hidden(weights, n, n // 2)

    parts = [
        first_section(blocked, inner_forward, twiddle_forward, s, n) for s in range(seqs)
    ]
    step = n // 2
    spread = []
    waits = [weights]
    for p in parts:
        last = exchange(after(p, *waits))
        spread.append(last.reshape(outer, -1, ch))
        if step > 1:
            step //= 2
            weights = more_hidden(weights, n, step)
        waits = [last, weights]
    out = None
    for s in range(seqs):
        groups = RETURN_ROWS[min(s, 1)]
        back = outer_section(
            spread[s], outer_forward, outer_inverse, twiddle_inverse, freq_kernel, groups, n
        )
        first = 0
        for part, count in zip(back, groups):
            part = exchange(after(part, *waits))
            waits = [part] if out is None else [part, out]
            if out is not None:
                part = after(part, out)
            while step > 1:
                step //= 2
                weights = more_hidden(weights, n, step)
                waits.append(weights)
            for skip in range(0, count, GATE_ROWS):
                size = min(GATE_ROWS, count - skip)
                gated, sq = gate_rows(
                    blocked, inner_inverse, gain, bias, part, s, first, skip, size
                )
                total = sq
                for r in range(1, n_ch):
                    total = total + lax.ppermute(
                        sq, "ch", [(j, (j + r) % n_ch) for j in range(n_ch)]
                    )
                for done in range(0, size, MLP_ROWS):
                    out = mlp_rows(
                        gated,
                        total,
                        norm,
                        weights,
                        out,
                        done,
                        min(MLP_ROWS, size - done),
                        s * a_dev + first + skip + done,
                        seqs * a_dev,
                        ch * n_ch,
                    )
            first += count
    return out.reshape(seqs, tok_dev, ch)


def local_rows(
    tokens,
    inner_forward,
    outer_forward,
    twiddle_forward,
    freq_kernel,
    outer_inverse,
    inner_inverse,
    twiddle_inverse,
    gate_gain,
    gate_bias,
    norm_gain,
    up_weight,
    down_weight,
):
    seq_total, tok_dev, ch_dev = tokens.shape
    inner_size = inner_forward.shape[0]
    outer_dev = tok_dev // inner_size
    blocked = tokens.reshape(seq_total, outer_dev, inner_size, ch_dev)
    section_one = jnp.einsum(
        "kb,xabc->xakc", inner_forward, blocked, preferred_element_type=jnp.float32
    )
    section_one = (section_one * twiddle_forward[None, :, :, None]).astype(jnp.bfloat16)
    spread = lax.all_to_all(section_one, "seq", split_axis=2, concat_axis=1, tiled=True)
    spectrum = jnp.einsum(
        "ka,xabc->xkbc", outer_forward, spread, preferred_element_type=jnp.float32
    )
    spectrum = (spectrum * freq_kernel[None].astype(jnp.float32)).astype(jnp.bfloat16)
    section_two = jnp.einsum(
        "nk,xkbc->xnbc", outer_inverse, spectrum, preferred_element_type=jnp.float32
    )
    section_two = (section_two * twiddle_inverse[None, :, :, None]).astype(jnp.bfloat16)
    gathered = lax.all_to_all(section_two, "seq", split_axis=1, concat_axis=2, tiled=True)
    block_count = up_weight.shape[0]
    width_block = up_weight.shape[2]
    mixed = jnp.einsum("mk,xakc->xamc", inner_inverse, gathered, preferred_element_type=jnp.float32)
    flat = blocked.astype(jnp.float32)
    gate = jax.nn.sigmoid(flat * gate_gain + gate_bias)
    gated = (flat + gate * mixed).astype(jnp.bfloat16)
    full_rows = lax.all_to_all(
        gated.reshape(blocked.shape[0], tok_dev, ch_dev),
        "ch",
        split_axis=1,
        concat_axis=2,
        tiled=True,
    )
    rows_dev = full_rows.shape[1]
    width = full_rows.shape[2]
    rows_f = full_rows.astype(jnp.float32)
    scale = lax.rsqrt(jnp.mean(rows_f * rows_f, axis=-1, keepdims=True) + EPS)
    normed = (rows_f * scale * norm_gain).astype(jnp.bfloat16)
    normed_b = normed.reshape(seq_total * rows_dev, block_count, width_block)
    lifted = jnp.einsum(
        "rbi,bji->rbj",
        normed_b,
        lax.all_gather(up_weight, "seq", axis=1, tiled=True),
        preferred_element_type=jnp.float32,
    )
    hidden = jax.nn.gelu(lifted, approximate=True).astype(jnp.bfloat16)
    lowered = jnp.einsum(
        "rbj,bji->rbi",
        hidden,
        lax.all_gather(down_weight, "seq", axis=1, tiled=True),
        preferred_element_type=jnp.float32,
    )
    result_rows = (rows_f + lowered.reshape(seq_total, rows_dev, width)).astype(jnp.bfloat16)
    return lax.all_to_all(result_rows, "ch", split_axis=2, concat_axis=1, tiled=True)


def local(*args):
    tokens, up_weight = args[0], args[11]
    n = lax.axis_size("seq")
    if tokens.shape[2] % up_weight.shape[2] == 0 and n & (n - 1) == 0:
        return local_blocks(*args)
    return local_rows(*args)


def solution(mesh):
    in_specs = (
        P(None, "seq", "ch"),
        P(),
        P(),
        P("seq", None),
        P(None, "seq", "ch"),
        P(),
        P(),
        P(None, "seq"),
        P("ch"),
        P("ch"),
        P(),
        P(None, "seq", None),
        P(None, "seq", None),
    )
    out_specs = P(None, "seq", "ch")
    return jax.shard_map(local, mesh=mesh, in_specs=in_specs, out_specs=out_specs, check_vma=False)
```

```python
import functools

import jax
import jax.numpy as jnp
from jax import lax
from jax.experimental import pallas as pl
from jax.experimental.pallas import tpu as pltpu
from jax.sharding import PartitionSpec as P

VMEM_BYTES = 32 * 1024 * 1024
EPS = 1e-06
RETURN_ROWS = ((8,), (6, 2))
STEP_ROWS = 2


def params():
    return pltpu.CompilerParams(vmem_limit_bytes=VMEM_BYTES)


def first_kernel(tok_ref, w_ref, tw_ref, out_ref):
    n, step, rows, ch = out_ref.shape
    cols = tw_ref[...].T
    lane = lax.broadcasted_iota(jnp.int32, cols.shape, 1)
    for j in range(step):
        a = pl.program_id(0) * step + j
        res = jnp.dot(w_ref[...], tok_ref[0, j], preferred_element_type=jnp.float32)
        tw = jnp.sum(jnp.where(lane == a, cols, 0.0), axis=1, keepdims=True)
        out_ref[:, j] = (res * tw).astype(jnp.bfloat16).reshape(n, rows, ch)


def first_section(blocked, inner_forward, twiddle, s, n):
    _, a_dev, inner, ch = blocked.shape
    rows = inner // n
    step = STEP_ROWS if a_dev % STEP_ROWS == 0 else 1
    return pl.pallas_call(
        first_kernel,
        grid=(a_dev // step,),
        in_specs=[
            pl.BlockSpec((1, step, inner, ch), lambda a: (s, a, 0, 0)),
            pl.BlockSpec((inner, inner), lambda a: (0, 0)),
            pl.BlockSpec((a_dev, inner), lambda a: (0, 0)),
        ],
        out_specs=pl.BlockSpec((n, step, rows, ch), lambda a: (0, a, 0, 0)),
        out_shape=jax.ShapeDtypeStruct((n, a_dev, rows, ch), jnp.bfloat16),
        compiler_params=params(),
        name="first_section",
    )(blocked, inner_forward, twiddle)


def outer_kernel(groups, fwd_ref, inv_ref, tw_ref, freq_ref, spread_ref, *rest):
    outs, (xs, fs, ys) = rest[:-3], rest[-3:]
    steps, outer, block = xs.shape
    xs[...] = jnp.swapaxes(spread_ref[...].astype(jnp.float32), 0, 1)
    fs[...] = jnp.swapaxes(freq_ref[...].astype(jnp.float32), 0, 1)
    tw = tw_ref[0]
    for k in range(steps):
        spectrum = jnp.dot(
            fwd_ref[...], xs[k].astype(jnp.bfloat16), preferred_element_type=jnp.float32
        )
        spectrum = (spectrum * fs[k]).astype(jnp.bfloat16)
        two = jnp.dot(inv_ref[...], spectrum, preferred_element_type=jnp.float32)
        ys[k] = two * tw[:, k : k + 1]
    res = jnp.swapaxes(ys[...], 0, 1).astype(jnp.bfloat16)
    n = outs[0].shape[0]
    res = res.reshape(n, outer // n, steps, block)
    first = 0
    for out, count in zip(outs, groups):
        out[...] = res[:, first : first + count]
        first += count


def outer_section(spread, forward, inverse, tw, freq, groups, n):
    outer, k_dev, ch = freq.shape
    rows, block = min(16, k_dev), min(256, ch)
    tw = tw.reshape(outer, k_dev // rows, rows).swapaxes(0, 1)
    return pl.pallas_call(
        functools.partial(outer_kernel, groups),
        grid=(k_dev // rows, ch // block),
        in_specs=[
            pl.BlockSpec((outer, outer), lambda h, c: (0, 0)),
            pl.BlockSpec((outer, outer), lambda h, c: (0, 0)),
            pl.BlockSpec((1, outer, rows), lambda h, c: (h, 0, 0)),
            pl.BlockSpec((outer, rows, block), lambda h, c: (0, h, c)),
            pl.BlockSpec((outer, rows, block), lambda h, c: (0, h, c)),
        ],
        out_specs=[
            pl.BlockSpec((n, count, rows, block), lambda h, c: (0, 0, h, c)) for count in groups
        ],
        out_shape=[
            jax.ShapeDtypeStruct((n, count, k_dev, ch), jnp.bfloat16) for count in groups
        ],
        scratch_shapes=[pltpu.VMEM((rows, outer, block), jnp.float32)] * 3,
        compiler_params=params(),
        name="outer_section",
    )(forward, inverse, tw, freq, spread)


def gate_kernel(tok_ref, w_ref, gain_ref, bias_ref, part_ref, gated_ref, sq_ref):
    flat = tok_ref[0, 0].astype(jnp.float32)
    section = part_ref[...].reshape(flat.shape)
    mixed = jnp.dot(w_ref[...], section, preferred_element_type=jnp.float32)
    gate = jax.nn.sigmoid(flat * gain_ref[...] + bias_ref[...])
    gated = (flat + gate * mixed).astype(jnp.bfloat16)
    gated_ref[0] = gated
    g = gated.astype(jnp.float32)
    sq = g * g
    part = sq[:, :128]
    for c in range(128, sq.shape[1], 128):
        part = part + sq[:, c : c + 128]
    sq_ref[0] = jnp.sum(part.T, axis=0, keepdims=True)


def gate_rows(blocked, inner_inverse, gain, bias, parts, s, first):
    _, _, inner, ch = blocked.shape
    n, count, rows, _ = parts.shape
    return pl.pallas_call(
        gate_kernel,
        grid=(count,),
        in_specs=[
            pl.BlockSpec((1, 1, inner, ch), lambda j: (s, first + j, 0, 0)),
            pl.BlockSpec((inner, inner), lambda j: (0, 0)),
            pl.BlockSpec((1, ch), lambda j: (0, 0)),
            pl.BlockSpec((1, ch), lambda j: (0, 0)),
            pl.BlockSpec((n, 1, rows, ch), lambda j: (0, j, 0, 0)),
        ],
        out_specs=[
            pl.BlockSpec((1, inner, ch), lambda j: (j, 0, 0)),
            pl.BlockSpec((1, 1, inner), lambda j: (j, 0, 0)),
        ],
        out_shape=[
            jax.ShapeDtypeStruct((count, inner, ch), jnp.bfloat16),
            jax.ShapeDtypeStruct((count, 1, inner), jnp.float32),
        ],
        compiler_params=params(),
        name="gate_rows",
    )(blocked, inner_inverse, gain, bias, parts)


def mlp_kernel(width, n_sq, gated_ref, gain_ref, weight_ref, *rest):
    out_ref = rest[-1]
    _, blocks, _, wb = weight_ref.shape
    total = rest[0][0]
    for sq_ref in rest[1:n_sq]:
        total = total + sq_ref[0]
    scale = lax.rsqrt(total * (1.0 / width) + EPS)
    scale = jnp.broadcast_to(scale, (128, scale.shape[1])).T[:, :1]
    for b in range(blocks):
        cols = slice(b * wb, (b + 1) * wb)
        g = gated_ref[0, :, cols].astype(jnp.float32)
        normed = (g * scale * gain_ref[:, cols]).astype(jnp.bfloat16)
        lifted = lax.dot_general(
            normed, weight_ref[0, b], (((1,), (1,)), ((), ())), preferred_element_type=jnp.float32
        )
        hidden = jax.nn.gelu(lifted, approximate=True).astype(jnp.bfloat16)
        lowered = jnp.dot(hidden, weight_ref[1, b], preferred_element_type=jnp.float32)
        out_ref[0, :, cols] = (g + lowered).astype(jnp.bfloat16)


def mlp_rows(gated, sqs, gain, weights, out, first, total, width):
    count, inner, ch = gated.shape
    specs = [
        pl.BlockSpec((1, inner, ch), lambda j: (j, 0, 0)),
        pl.BlockSpec((1, ch), lambda j: (0, 0)),
        pl.BlockSpec(memory_space=pltpu.VMEM),
    ] + [pl.BlockSpec((1, 1, inner), lambda j: (j, 0, 0))] * len(sqs)
    args = [gated, gain, weights, *sqs]
    aliases = {}
    if out is not None:
        aliases = {len(args): 0}
        specs.append(pl.BlockSpec(memory_space=pl.ANY))
        args.append(out)
    return pl.pallas_call(
        functools.partial(mlp_kernel, width, len(sqs)),
        grid=(count,),
        in_specs=specs,
        out_specs=pl.BlockSpec((1, inner, ch), lambda j: (first + j, 0, 0)),
        out_shape=jax.ShapeDtypeStruct((total, inner, ch), jnp.bfloat16),
        input_output_aliases=aliases,
        compiler_params=params(),
        name="mlp_rows",
    )(*args)


def after(x, *deps):
    return lax.optimization_barrier((x,) + deps)[0]


def after(x, *deps):
    return lax.optimization_barrier((x,) + deps)[0]


def exchange(x):
    return lax.all_to_all(x, "seq", split_axis=0, concat_axis=0, tiled=True)


def more_hidden(weights, n, step):
    other = lax.ppermute(weights, "seq", [(j, j ^ step) for j in range(n)])
    return jnp.concatenate([weights, other], axis=2)


def local_blocks(
    tokens,
    inner_forward,
    outer_forward,
    twiddle_forward,
    freq_kernel,
    outer_inverse,
    inner_inverse,
    twiddle_inverse,
    gate_gain,
    gate_bias,
    norm_gain,
    up_weight,
    down_weight,
):

    seqs, tok_dev, ch = tokens.shape
    inner = inner_forward.shape[0]
    a_dev = tok_dev // inner
    n = lax.axis_size("seq")
    n_ch = lax.axis_size("ch")
    my_ch = lax.axis_index("ch")
    outer = n * a_dev
    blocked = tokens.reshape(seqs, a_dev, inner, ch)
    norm = lax.dynamic_slice_in_dim(norm_gain, my_ch * ch, ch, 0).reshape(1, ch)
    gain, bias = gate_gain.reshape(1, ch), gate_bias.reshape(1, ch)
    held = ch // up_weight.shape[2]
    weights = lax.dynamic_slice_in_dim(
        jnp.stack([up_weight, down_weight]), my_ch * held, held, 1
    )
    weights = more_hidden(weights, n, n // 2)

    parts = [
        first_section(blocked, inner_forward, twiddle_forward, s, n) for s in range(seqs)
    ]
    step = n // 2
    spread = []
    waits = [weights]
    for p in parts:
        last = exchange(after(p, *waits))
        spread.append(last.reshape(outer, -1, ch))
        if step > 1:
            step //= 2
            weights = more_hidden(weights, n, step)
        waits = [last, weights]
    out = None
    for s in range(seqs):
        groups = RETURN_ROWS[min(s, 1)]
        back = outer_section(
            spread[s], outer_forward, outer_inverse, twiddle_inverse, freq_kernel, groups, n
        )
        first = 0
        for part, count in zip(back, groups):
            part = exchange(after(part, *waits))
            waits = [part] if out is None else [part, out]
            if out is not None:
                part = after(part, out)
            while step > 1:
                step //= 2
                weights = more_hidden(weights, n, step)
                waits.append(weights)
            gated, sq = gate_rows(blocked, inner_inverse, gain, bias, part, s, first)
            sqs = [sq] + [
                lax.ppermute(sq, "ch", [(j, (j + r) % n_ch) for j in range(n_ch)])
                for r in range(1, n_ch)
            ]
            out = mlp_rows(
                gated, sqs, norm, weights, out, s * a_dev + first, seqs * a_dev, ch * n_ch
            )
            first += count
    return out.reshape(seqs, tok_dev, ch)


def local_rows(
    tokens,
    inner_forward,
    outer_forward,
    twiddle_forward,
    freq_kernel,
    outer_inverse,
    inner_inverse,
    twiddle_inverse,
    gate_gain,
    gate_bias,
    norm_gain,
    up_weight,
    down_weight,
):
    seq_total, tok_dev, ch_dev = tokens.shape
    inner_size = inner_forward.shape[0]
    outer_dev = tok_dev // inner_size
    blocked = tokens.reshape(seq_total, outer_dev, inner_size, ch_dev)
    section_one = jnp.einsum(
        "kb,xabc->xakc", inner_forward, blocked, preferred_element_type=jnp.float32
    )
    section_one = (section_one * twiddle_forward[None, :, :, None]).astype(jnp.bfloat16)
    spread = lax.all_to_all(section_one, "seq", split_axis=2, concat_axis=1, tiled=True)
    spectrum = jnp.einsum(
        "ka,xabc->xkbc", outer_forward, spread, preferred_element_type=jnp.float32
    )
    spectrum = (spectrum * freq_kernel[None].astype(jnp.float32)).astype(jnp.bfloat16)
    section_two = jnp.einsum(
        "nk,xkbc->xnbc", outer_inverse, spectrum, preferred_element_type=jnp.float32
    )
    section_two = (section_two * twiddle_inverse[None, :, :, None]).astype(jnp.bfloat16)
    gathered = lax.all_to_all(section_two, "seq", split_axis=1, concat_axis=2, tiled=True)
    block_count = up_weight.shape[0]
    width_block = up_weight.shape[2]
    mixed = jnp.einsum("mk,xakc->xamc", inner_inverse, gathered, preferred_element_type=jnp.float32)
    flat = blocked.astype(jnp.float32)
    gate = jax.nn.sigmoid(flat * gate_gain + gate_bias)
    gated = (flat + gate * mixed).astype(jnp.bfloat16)
    full_rows = lax.all_to_all(
        gated.reshape(blocked.shape[0], tok_dev, ch_dev),
        "ch",
        split_axis=1,
        concat_axis=2,
        tiled=True,
    )
    rows_dev = full_rows.shape[1]
    width = full_rows.shape[2]
    rows_f = full_rows.astype(jnp.float32)
    scale = lax.rsqrt(jnp.mean(rows_f * rows_f, axis=-1, keepdims=True) + EPS)
    normed = (rows_f * scale * norm_gain).astype(jnp.bfloat16)
    normed_b = normed.reshape(seq_total * rows_dev, block_count, width_block)
    lifted = jnp.einsum(
        "rbi,bji->rbj",
        normed_b,
        lax.all_gather(up_weight, "seq", axis=1, tiled=True),
        preferred_element_type=jnp.float32,
    )
    hidden = jax.nn.gelu(lifted, approximate=True).astype(jnp.bfloat16)
    lowered = jnp.einsum(
        "rbj,bji->rbi",
        hidden,
        lax.all_gather(down_weight, "seq", axis=1, tiled=True),
        preferred_element_type=jnp.float32,
    )
    result_rows = (rows_f + lowered.reshape(seq_total, rows_dev, width)).astype(jnp.bfloat16)
    return lax.all_to_all(result_rows, "ch", split_axis=2, concat_axis=1, tiled=True)


def local(*args):
    tokens, up_weight = args[0], args[11]
    n = lax.axis_size("seq")
    if tokens.shape[2] % up_weight.shape[2] == 0 and n & (n - 1) == 0:
        return local_blocks(*args)
    return local_rows(*args)


def solution(mesh):
    in_specs = (
        P(None, "seq", "ch"),
        P(),
        P(),
        P("seq", None),
        P(None, "seq", "ch"),
        P(),
        P(),
        P(None, "seq"),
        P("ch"),
        P("ch"),
        P(),
        P(None, "seq", None),
        P(None, "seq", None),
    )
    out_specs = P(None, "seq", "ch")
    return jax.shard_map(local, mesh=mesh, in_specs=in_specs, out_specs=out_specs, check_vma=False)
```

```python
import functools

import jax
import jax.numpy as jnp
from jax import lax
from jax.experimental import pallas as pl
from jax.experimental.pallas import tpu as pltpu
from jax.sharding import PartitionSpec as P

VMEM_BYTES = 32 * 1024 * 1024
EPS = 1e-06
STEP_ROWS = 2
LAST_ROWS = 2


def params(size=VMEM_BYTES):
    return pltpu.CompilerParams(vmem_limit_bytes=size)


def first_kernel(tok_ref, w_ref, tw_ref, out_ref):
    n, step, rows, ch = out_ref.shape
    cols = tw_ref[...].T
    lane = lax.broadcasted_iota(jnp.int32, cols.shape, 1)
    for j in range(step):
        a = pl.program_id(0) * step + j
        res = jnp.dot(w_ref[...], tok_ref[0, j], preferred_element_type=jnp.float32)
        tw = jnp.sum(jnp.where(lane == a, cols, 0.0), axis=1, keepdims=True)
        out_ref[:, j] = (res * tw).astype(jnp.bfloat16).reshape(n, rows, ch)


def first_section(blocked, inner_forward, twiddle, s, n):
    _, a_dev, inner, ch = blocked.shape
    rows = inner // n
    step = STEP_ROWS if a_dev % STEP_ROWS == 0 else 1
    return pl.pallas_call(
        first_kernel,
        grid=(a_dev // step,),
        in_specs=[
            pl.BlockSpec((1, step, inner, ch), lambda a: (s, a, 0, 0)),
            pl.BlockSpec((inner, inner), lambda a: (0, 0)),
            pl.BlockSpec((a_dev, inner), lambda a: (0, 0)),
        ],
        out_specs=pl.BlockSpec((n, step, rows, ch), lambda a: (0, a, 0, 0)),
        out_shape=jax.ShapeDtypeStruct((n, a_dev, rows, ch), jnp.bfloat16),
        compiler_params=params(),
        name="first_section",
    )(blocked, inner_forward, twiddle)


def outer_kernel(groups, fwd_ref, inv_ref, tw_ref, freq_ref, spread_ref, *rest):
    outs, (xs, fs, ys) = rest[:-3], rest[-3:]
    steps, outer, block = xs.shape
    xs[...] = jnp.swapaxes(spread_ref[...].astype(jnp.float32), 0, 1)
    fs[...] = jnp.swapaxes(freq_ref[...].astype(jnp.float32), 0, 1)
    tw = tw_ref[0]
    for k in range(steps):
        spectrum = jnp.dot(
            fwd_ref[...], xs[k].astype(jnp.bfloat16), preferred_element_type=jnp.float32
        )
        spectrum = (spectrum * fs[k]).astype(jnp.bfloat16)
        two = jnp.dot(inv_ref[...], spectrum, preferred_element_type=jnp.float32)
        ys[k] = two * tw[:, k : k + 1]
    res = jnp.swapaxes(ys[...], 0, 1).astype(jnp.bfloat16)
    n = outs[0].shape[0]
    res = res.reshape(n, outer // n, steps, block)
    first = 0
    for out, count in zip(outs, groups):
        out[...] = res[:, first : first + count]
        first += count


def outer_section(spread, forward, inverse, tw, freq, groups, n):
    outer, k_dev, ch = freq.shape
    rows, block = min(16, k_dev), min(256, ch)
    tw = tw.reshape(outer, k_dev // rows, rows).swapaxes(0, 1)
    return pl.pallas_call(
        functools.partial(outer_kernel, groups),
        grid=(k_dev // rows, ch // block),
        in_specs=[
            pl.BlockSpec((outer, outer), lambda h, c: (0, 0)),
            pl.BlockSpec((outer, outer), lambda h, c: (0, 0)),
            pl.BlockSpec((1, outer, rows), lambda h, c: (h, 0, 0)),
            pl.BlockSpec((outer, rows, block), lambda h, c: (0, h, c)),
            pl.BlockSpec((outer, rows, block), lambda h, c: (0, h, c)),
        ],
        out_specs=[
            pl.BlockSpec((n, count, rows, block), lambda h, c: (0, 0, h, c)) for count in groups
        ],
        out_shape=[
            jax.ShapeDtypeStruct((n, count, k_dev, ch), jnp.bfloat16) for count in groups
        ],
        scratch_shapes=[pltpu.VMEM((rows, outer, block), jnp.float32)] * 3,
        compiler_params=params(),
        name="outer_section",
    )(forward, inverse, tw, freq, spread)


def gate_kernel(tok_ref, w_ref, gain_ref, bias_ref, part_ref, gated_ref, sq_ref):
    flat = tok_ref[0, 0].astype(jnp.float32)
    section = part_ref[...].reshape(flat.shape)
    mixed = jnp.dot(w_ref[...], section, preferred_element_type=jnp.float32)
    gate = jax.nn.sigmoid(flat * gain_ref[...] + bias_ref[...])
    gated = (flat + gate * mixed).astype(jnp.bfloat16)
    gated_ref[0] = gated
    g = gated.astype(jnp.float32)
    sq = g * g
    part = sq[:, :128]
    for c in range(128, sq.shape[1], 128):
        part = part + sq[:, c : c + 128]
    sq_ref[0] = jnp.sum(part.T, axis=0, keepdims=True)


def gate_rows(blocked, inner_inverse, gain, bias, parts, s, first):
    _, _, inner, ch = blocked.shape
    n, count, rows, _ = parts.shape
    return pl.pallas_call(
        gate_kernel,
        grid=(count,),
        in_specs=[
            pl.BlockSpec((1, 1, inner, ch), lambda j: (s, first + j, 0, 0)),
            pl.BlockSpec((inner, inner), lambda j: (0, 0)),
            pl.BlockSpec((1, ch), lambda j: (0, 0)),
            pl.BlockSpec((1, ch), lambda j: (0, 0)),
            pl.BlockSpec((n, 1, rows, ch), lambda j: (0, j, 0, 0)),
        ],
        out_specs=[
            pl.BlockSpec((1, inner, ch), lambda j: (j, 0, 0)),
            pl.BlockSpec((1, 1, inner), lambda j: (j, 0, 0)),
        ],
        out_shape=[
            jax.ShapeDtypeStruct((count, inner, ch), jnp.bfloat16),
            jax.ShapeDtypeStruct((count, 1, inner), jnp.float32),
        ],
        compiler_params=params(),
        name="gate_rows",
    )(blocked, inner_inverse, gain, bias, parts)


def mlp_kernel(width, n_sq, gated_ref, gain_ref, weight_ref, *rest):
    out_ref = rest[-1]
    _, blocks, _, wb = weight_ref.shape
    total = rest[0][0]
    for sq_ref in rest[1:n_sq]:
        total = total + sq_ref[0]
    scale = lax.rsqrt(total * (1.0 / width) + EPS)
    scale = jnp.broadcast_to(scale, (128, scale.shape[1])).T[:, :1]
    for b in range(blocks):
        cols = slice(b * wb, (b + 1) * wb)
        g = gated_ref[0, :, cols].astype(jnp.float32)
        normed = (g * scale * gain_ref[:, cols]).astype(jnp.bfloat16)
        lifted = lax.dot_general(
            normed, weight_ref[0, b], (((1,), (1,)), ((), ())), preferred_element_type=jnp.float32
        )
        hidden = jax.nn.gelu(lifted, approximate=True).astype(jnp.bfloat16)
        lowered = jnp.dot(hidden, weight_ref[1, b], preferred_element_type=jnp.float32)
        out_ref[0, :, cols] = (g + lowered).astype(jnp.bfloat16)


def mlp_rows(gated, sqs, gain, weights, out, first, total, width):
    count, inner, ch = gated.shape
    specs = [
        pl.BlockSpec((1, inner, ch), lambda j: (j, 0, 0)),
        pl.BlockSpec((1, ch), lambda j: (0, 0)),
        pl.BlockSpec(memory_space=pltpu.VMEM),
    ] + [pl.BlockSpec((1, 1, inner), lambda j: (j, 0, 0))] * len(sqs)
    args = [gated, gain, weights, *sqs]
    aliases = {}
    if out is not None:
        aliases = {len(args): 0}
        specs.append(pl.BlockSpec(memory_space=pl.ANY))
        args.append(out)
    return pl.pallas_call(
        functools.partial(mlp_kernel, width, len(sqs)),
        grid=(count,),
        in_specs=specs,
        out_specs=pl.BlockSpec((1, inner, ch), lambda j: (first + j, 0, 0)),
        out_shape=jax.ShapeDtypeStruct((total, inner, ch), jnp.bfloat16),
        input_output_aliases=aliases,
        compiler_params=params(),
        name="mlp_rows",
    )(*args)


def after(x, *deps):
    return lax.optimization_barrier((x,) + deps)[0]


def exchange(x):
    return lax.all_to_all(x, "seq", split_axis=0, concat_axis=0, tiled=True)


def more_hidden(weights, n, step):
    other = lax.ppermute(weights, "seq", [(j, j ^ step) for j in range(n)])
    return jnp.concatenate([weights, other], axis=2)


def local_blocks(
    tokens,
    inner_forward,
    outer_forward,
    twiddle_forward,
    freq_kernel,
    outer_inverse,
    inner_inverse,
    twiddle_inverse,
    gate_gain,
    gate_bias,
    norm_gain,
    up_weight,
    down_weight,
):
    seqs, tok_dev, ch = tokens.shape
    inner = inner_forward.shape[0]
    a_dev = tok_dev // inner
    n = lax.axis_size("seq")
    n_ch = lax.axis_size("ch")
    my_ch = lax.axis_index("ch")
    outer = n * a_dev
    blocked = tokens.reshape(seqs, a_dev, inner, ch)
    norm = lax.dynamic_slice_in_dim(norm_gain, my_ch * ch, ch, 0).reshape(1, ch)
    gain, bias = gate_gain.reshape(1, ch), gate_bias.reshape(1, ch)
    held = ch // up_weight.shape[2]
    weights = lax.dynamic_slice_in_dim(
        jnp.stack([up_weight, down_weight]), my_ch * held, held, 1
    )
    weights = more_hidden(weights, n, n // 2)

    parts = [
        first_section(blocked, inner_forward, twiddle_forward, s, n) for s in range(seqs)
    ]
    step = n // 2
    spread = []
    waits = [weights]
    for p in parts:
        last = exchange(after(p, *waits))
        spread.append(last.reshape(outer, -1, ch))
        if step > 1:
            step //= 2
            weights = more_hidden(weights, n, step)
        waits = [last, weights]
    out = None
    for s in range(seqs):
        last_rows = LAST_ROWS if s + 1 == seqs and a_dev > LAST_ROWS else 0
        groups = (a_dev - last_rows, last_rows) if last_rows else (a_dev,)
        back = outer_section(
            spread[s], outer_forward, outer_inverse, twiddle_inverse, freq_kernel, groups, n
        )
        first = 0
        for part, count in zip(back, groups):
            part = exchange(after(part, *waits))
            waits = [part] if out is None else [part, out]
            if out is not None:
                part = after(part, out)
            while step > 1:
                step //= 2
                weights = more_hidden(weights, n, step)
                waits.append(weights)
            gated, sq = gate_rows(blocked, inner_inverse, gain, bias, part, s, first)
            sqs = [sq] + [
                lax.ppermute(sq, "ch", [(j, (j + r) % n_ch) for j in range(n_ch)])
                for r in range(1, n_ch)
            ]
            out = mlp_rows(
                gated, sqs, norm, weights, out, s * a_dev + first, seqs * a_dev, ch * n_ch
            )
            first += count
    return out.reshape(seqs, tok_dev, ch)


def local_rows(
    tokens,
    inner_forward,
    outer_forward,
    twiddle_forward,
    freq_kernel,
    outer_inverse,
    inner_inverse,
    twiddle_inverse,
    gate_gain,
    gate_bias,
    norm_gain,
    up_weight,
    down_weight,
):
    seq_total, tok_dev, ch_dev = tokens.shape
    inner_size = inner_forward.shape[0]
    outer_dev = tok_dev // inner_size
    blocked = tokens.reshape(seq_total, outer_dev, inner_size, ch_dev)
    section_one = jnp.einsum(
        "kb,xabc->xakc", inner_forward, blocked, preferred_element_type=jnp.float32
    )
    section_one = (section_one * twiddle_forward[None, :, :, None]).astype(jnp.bfloat16)
    spread = lax.all_to_all(section_one, "seq", split_axis=2, concat_axis=1, tiled=True)
    spectrum = jnp.einsum(
        "ka,xabc->xkbc", outer_forward, spread, preferred_element_type=jnp.float32
    )
    spectrum = (spectrum * freq_kernel[None].astype(jnp.float32)).astype(jnp.bfloat16)
    section_two = jnp.einsum(
        "nk,xkbc->xnbc", outer_inverse, spectrum, preferred_element_type=jnp.float32
    )
    section_two = (section_two * twiddle_inverse[None, :, :, None]).astype(jnp.bfloat16)
    gathered = lax.all_to_all(section_two, "seq", split_axis=1, concat_axis=2, tiled=True)
    block_count = up_weight.shape[0]
    width_block = up_weight.shape[2]
    mixed = jnp.einsum("mk,xakc->xamc", inner_inverse, gathered, preferred_element_type=jnp.float32)
    flat = blocked.astype(jnp.float32)
    gate = jax.nn.sigmoid(flat * gate_gain + gate_bias)
    gated = (flat + gate * mixed).astype(jnp.bfloat16)
    full_rows = lax.all_to_all(
        gated.reshape(blocked.shape[0], tok_dev, ch_dev),
        "ch",
        split_axis=1,
        concat_axis=2,
        tiled=True,
    )
    rows_dev = full_rows.shape[1]
    width = full_rows.shape[2]
    rows_f = full_rows.astype(jnp.float32)
    scale = lax.rsqrt(jnp.mean(rows_f * rows_f, axis=-1, keepdims=True) + EPS)
    normed = (rows_f * scale * norm_gain).astype(jnp.bfloat16)
    normed_b = normed.reshape(seq_total * rows_dev, block_count, width_block)
    lifted = jnp.einsum(
        "rbi,bji->rbj",
        normed_b,
        lax.all_gather(up_weight, "seq", axis=1, tiled=True),
        preferred_element_type=jnp.float32,
    )
    hidden = jax.nn.gelu(lifted, approximate=True).astype(jnp.bfloat16)
    lowered = jnp.einsum(
        "rbj,bji->rbi",
        hidden,
        lax.all_gather(down_weight, "seq", axis=1, tiled=True),
        preferred_element_type=jnp.float32,
    )
    result_rows = (rows_f + lowered.reshape(seq_total, rows_dev, width)).astype(jnp.bfloat16)
    return lax.all_to_all(result_rows, "ch", split_axis=2, concat_axis=1, tiled=True)


def local(*args):
    tokens, up_weight = args[0], args[11]
    n = lax.axis_size("seq")
    if tokens.shape[2] % up_weight.shape[2] == 0 and n & (n - 1) == 0:
        return local_blocks(*args)
    return local_rows(*args)


def solution(mesh):
    in_specs = (
        P(None, "seq", "ch"),
        P(),
        P(),
        P("seq", None),
        P(None, "seq", "ch"),
        P(),
        P(),
        P(None, "seq"),
        P("ch"),
        P("ch"),
        P(),
        P(None, "seq", None),
        P(None, "seq", None),
    )
    out_specs = P(None, "seq", "ch")
    return jax.shard_map(local, mesh=mesh, in_specs=in_specs, out_specs=out_specs, check_vma=False)
```

```python
import functools

import jax
import jax.numpy as jnp
from jax import lax
from jax.experimental import pallas as pl
from jax.experimental.pallas import tpu as pltpu
from jax.sharding import PartitionSpec as P

VMEM_BYTES = 32 * 1024 * 1024
MOST_VMEM_BYTES = 56 * 1024 * 1024
GATE_VMEM_BYTES = 48 * 1024 * 1024
EPS = 1e-06
STEP_ROWS = 2
LAST_ROWS = 2


def params(size=VMEM_BYTES):
    return pltpu.CompilerParams(vmem_limit_bytes=size)


def first_kernel(tok_ref, w_ref, tw_ref, out_ref):
    n, step, rows, ch = out_ref.shape
    cols = tw_ref[...].T
    lane = lax.broadcasted_iota(jnp.int32, cols.shape, 1)
    for j in range(step):
        a = pl.program_id(0) * step + j
        res = jnp.dot(w_ref[...], tok_ref[0, j], preferred_element_type=jnp.float32)
        tw = jnp.sum(jnp.where(lane == a, cols, 0.0), axis=1, keepdims=True)
        out_ref[:, j] = (res * tw).astype(jnp.bfloat16).reshape(n, rows, ch)


def first_section(blocked, inner_forward, twiddle, s, n):
    _, a_dev, inner, ch = blocked.shape
    rows = inner // n
    step = STEP_ROWS if a_dev % STEP_ROWS == 0 else 1
    return pl.pallas_call(
        first_kernel,
        grid=(a_dev // step,),
        in_specs=[
            pl.BlockSpec((1, step, inner, ch), lambda a: (s, a, 0, 0)),
            pl.BlockSpec((inner, inner), lambda a: (0, 0)),
            pl.BlockSpec((a_dev, inner), lambda a: (0, 0)),
        ],
        out_specs=pl.BlockSpec((n, step, rows, ch), lambda a: (0, a, 0, 0)),
        out_shape=jax.ShapeDtypeStruct((n, a_dev, rows, ch), jnp.bfloat16),
        compiler_params=params(MOST_VMEM_BYTES),
        name="first_section",
    )(blocked, inner_forward, twiddle)


def outer_kernel(groups, fwd_ref, inv_ref, tw_ref, freq_ref, spread_ref, *rest):
    outs, (xs, fs, ys) = rest[:-3], rest[-3:]
    steps, outer, block = xs.shape
    xs[...] = jnp.swapaxes(spread_ref[...].astype(jnp.float32), 0, 1)
    fs[...] = jnp.swapaxes(freq_ref[...].astype(jnp.float32), 0, 1)
    tw = tw_ref[0]
    for k in range(steps):
        spectrum = jnp.dot(
            fwd_ref[...], xs[k].astype(jnp.bfloat16), preferred_element_type=jnp.float32
        )
        spectrum = (spectrum * fs[k]).astype(jnp.bfloat16)
        two = jnp.dot(inv_ref[...], spectrum, preferred_element_type=jnp.float32)
        ys[k] = two * tw[:, k : k + 1]
    res = jnp.swapaxes(ys[...], 0, 1).astype(jnp.bfloat16)
    n = outs[0].shape[0]
    res = res.reshape(n, outer // n, steps, block)
    first = 0
    for out, count in zip(outs, groups):
        out[...] = res[:, first : first + count]
        first += count


def outer_section(spread, forward, inverse, tw, freq, groups, n):
    outer, k_dev, ch = freq.shape
    rows, block = min(16, k_dev), min(256, ch)
    tw = tw.reshape(outer, k_dev // rows, rows).swapaxes(0, 1)
    return pl.pallas_call(
        functools.partial(outer_kernel, groups),
        grid=(k_dev // rows, ch // block),
        in_specs=[
            pl.BlockSpec((outer, outer), lambda h, c: (0, 0)),
            pl.BlockSpec((outer, outer), lambda h, c: (0, 0)),
            pl.BlockSpec((1, outer, rows), lambda h, c: (h, 0, 0)),
            pl.BlockSpec((outer, rows, block), lambda h, c: (0, h, c)),
            pl.BlockSpec((outer, rows, block), lambda h, c: (0, h, c)),
        ],
        out_specs=[
            pl.BlockSpec((n, count, rows, block), lambda h, c: (0, 0, h, c)) for count in groups
        ],
        out_shape=[
            jax.ShapeDtypeStruct((n, count, k_dev, ch), jnp.bfloat16) for count in groups
        ],
        scratch_shapes=[pltpu.VMEM((rows, outer, block), jnp.float32)] * 3,
        compiler_params=params(),
        name="outer_section",
    )(forward, inverse, tw, freq, spread)


def gate_kernel(tok_ref, w_ref, gain_ref, bias_ref, part_ref, gated_ref, sq_ref):
    flat = tok_ref[0, 0].astype(jnp.float32)
    section = part_ref[...].reshape(flat.shape)
    mixed = jnp.dot(w_ref[...], section, preferred_element_type=jnp.float32)
    gate = jax.nn.sigmoid(flat * gain_ref[...] + bias_ref[...])
    gated = (flat + gate * mixed).astype(jnp.bfloat16)
    gated_ref[0] = gated
    g = gated.astype(jnp.float32)
    sq = g * g
    part = sq[:, :128]
    for c in range(128, sq.shape[1], 128):
        part = part + sq[:, c : c + 128]
    sq_ref[0] = jnp.sum(part.T, axis=0, keepdims=True)


def gate_rows(blocked, inner_inverse, gain, bias, parts, s, first):
    _, _, inner, ch = blocked.shape
    n, count, rows, _ = parts.shape
    return pl.pallas_call(
        gate_kernel,
        grid=(count,),
        in_specs=[
            pl.BlockSpec((1, 1, inner, ch), lambda j: (s, first + j, 0, 0)),
            pl.BlockSpec((inner, inner), lambda j: (0, 0)),
            pl.BlockSpec((1, ch), lambda j: (0, 0)),
            pl.BlockSpec((1, ch), lambda j: (0, 0)),
            pl.BlockSpec((n, 1, rows, ch), lambda j: (0, j, 0, 0)),
        ],
        out_specs=[
            pl.BlockSpec((1, inner, ch), lambda j: (j, 0, 0)),
            pl.BlockSpec((1, 1, inner), lambda j: (j, 0, 0)),
        ],
        out_shape=[
            jax.ShapeDtypeStruct((count, inner, ch), jnp.bfloat16),
            jax.ShapeDtypeStruct((count, 1, inner), jnp.float32),
        ],
        compiler_params=params(GATE_VMEM_BYTES),
        name="gate_rows",
    )(blocked, inner_inverse, gain, bias, parts)


def mlp_kernel(width, n_sq, gated_ref, gain_ref, up_ref, down_ref, *rest):
    out_ref = rest[-1]
    blocks, _, wb = up_ref.shape
    total = rest[0][0]
    for sq_ref in rest[1:n_sq]:
        total = total + sq_ref[0]
    scale = lax.rsqrt(total * (1.0 / width) + EPS)
    scale = jnp.broadcast_to(scale, (128, scale.shape[1])).T[:, :1]
    for b in range(blocks):
        cols = slice(b * wb, (b + 1) * wb)
        g = gated_ref[0, :, cols].astype(jnp.float32)
        normed = (g * scale * gain_ref[:, cols]).astype(jnp.bfloat16)
        lifted = lax.dot_general(
            normed, up_ref[b], (((1,), (1,)), ((), ())), preferred_element_type=jnp.float32
        )
        hidden = jax.nn.gelu(lifted, approximate=True).astype(jnp.bfloat16)
        lowered = jnp.dot(hidden, down_ref[b], preferred_element_type=jnp.float32)
        out_ref[0, :, cols] = (g + lowered).astype(jnp.bfloat16)


def mlp_rows(gated, sqs, gain, weights, out, first, total, width):
    count, inner, ch = gated.shape
    specs = [
        pl.BlockSpec((1, inner, ch), lambda j: (j, 0, 0)),
        pl.BlockSpec((1, ch), lambda j: (0, 0)),
        pl.BlockSpec(memory_space=pltpu.VMEM),
        pl.BlockSpec(memory_space=pltpu.VMEM),
    ] + [pl.BlockSpec((1, 1, inner), lambda j: (j, 0, 0))] * len(sqs)
    args = [gated, gain, *weights, *sqs]
    aliases = {}
    if out is not None:
        aliases = {len(args): 0}
        specs.append(pl.BlockSpec(memory_space=pl.ANY))
        args.append(out)
    return pl.pallas_call(
        functools.partial(mlp_kernel, width, len(sqs)),
        grid=(count,),
        in_specs=specs,
        out_specs=pl.BlockSpec((1, inner, ch), lambda j: (first + j, 0, 0)),
        out_shape=jax.ShapeDtypeStruct((total, inner, ch), jnp.bfloat16),
        input_output_aliases=aliases,
        compiler_params=params(),
        name="mlp_rows",
    )(*args)


def after(x, *deps):
    return lax.optimization_barrier((x,) + deps)[0]


def exchange(x):
    return lax.all_to_all(x, "seq", split_axis=0, concat_axis=0, tiled=True)


def more_hidden(weights, n, step):
    pairs = [(j, j ^ step) for j in range(n)]
    return [jnp.concatenate([w, lax.ppermute(w, "seq", pairs)], axis=1) for w in weights]


def local_blocks(
    tokens,
    inner_forward,
    outer_forward,
    twiddle_forward,
    freq_kernel,
    outer_inverse,
    inner_inverse,
    twiddle_inverse,
    gate_gain,
    gate_bias,
    norm_gain,
    up_weight,
    down_weight,
):
    seqs, tok_dev, ch = tokens.shape
    inner = inner_forward.shape[0]
    a_dev = tok_dev // inner
    n = lax.axis_size("seq")
    n_ch = lax.axis_size("ch")
    my_ch = lax.axis_index("ch")
    outer = n * a_dev
    blocked = tokens.reshape(seqs, a_dev, inner, ch)
    norm = lax.dynamic_slice_in_dim(norm_gain, my_ch * ch, ch, 0).reshape(1, ch)
    gain, bias = gate_gain.reshape(1, ch), gate_bias.reshape(1, ch)
    held = ch // up_weight.shape[2]
    weights = [
        lax.dynamic_slice_in_dim(w, my_ch * held, held, 0) for w in (up_weight, down_weight)
    ]
    weights = more_hidden(weights, n, n // 2)

    parts = [
        first_section(blocked, inner_forward, twiddle_forward, s, n) for s in range(seqs)
    ]
    step = n // 2
    spread = []
    waits = weights
    for p in parts:
        last = exchange(after(p, *waits))
        spread.append(last.reshape(outer, -1, ch))
        if step > 1:
            step //= 2
            weights = more_hidden(weights, n, step)
        waits = [last, *weights]
    out = None
    for s in range(seqs):
        last_rows = LAST_ROWS if s + 1 == seqs and a_dev > LAST_ROWS else 0
        groups = (a_dev - last_rows, last_rows) if last_rows else (a_dev,)
        back = outer_section(
            spread[s], outer_forward, outer_inverse, twiddle_inverse, freq_kernel, groups, n
        )
        first = 0
        for part, count in zip(back, groups):
            part = exchange(after(part, *waits))
            waits = [part] if out is None else [part, out]
            if out is not None:
                part = after(part, out)
            while step > 1:
                step //= 2
                weights = more_hidden(weights, n, step)
                waits += weights
            gated, sq = gate_rows(blocked, inner_inverse, gain, bias, part, s, first)
            sqs = [sq] + [
                lax.ppermute(sq, "ch", [(j, (j + r) % n_ch) for j in range(n_ch)])
                for r in range(1, n_ch)
            ]
            out = mlp_rows(
                gated, sqs, norm, weights, out, s * a_dev + first, seqs * a_dev, ch * n_ch
            )
            first += count
    return out.reshape(seqs, tok_dev, ch)


def local_rows(
    tokens,
    inner_forward,
    outer_forward,
    twiddle_forward,
    freq_kernel,
    outer_inverse,
    inner_inverse,
    twiddle_inverse,
    gate_gain,
    gate_bias,
    norm_gain,
    up_weight,
    down_weight,
):
    seq_total, tok_dev, ch_dev = tokens.shape
    inner_size = inner_forward.shape[0]
    outer_dev = tok_dev // inner_size
    blocked = tokens.reshape(seq_total, outer_dev, inner_size, ch_dev)
    section_one = jnp.einsum(
        "kb,xabc->xakc", inner_forward, blocked, preferred_element_type=jnp.float32
    )
    section_one = (section_one * twiddle_forward[None, :, :, None]).astype(jnp.bfloat16)
    spread = lax.all_to_all(section_one, "seq", split_axis=2, concat_axis=1, tiled=True)
    spectrum = jnp.einsum(
        "ka,xabc->xkbc", outer_forward, spread, preferred_element_type=jnp.float32
    )
    spectrum = (spectrum * freq_kernel[None].astype(jnp.float32)).astype(jnp.bfloat16)
    section_two = jnp.einsum(
        "nk,xkbc->xnbc", outer_inverse, spectrum, preferred_element_type=jnp.float32
    )
    section_two = (section_two * twiddle_inverse[None, :, :, None]).astype(jnp.bfloat16)
    gathered = lax.all_to_all(section_two, "seq", split_axis=1, concat_axis=2, tiled=True)
    block_count = up_weight.shape[0]
    width_block = up_weight.shape[2]
    mixed = jnp.einsum("mk,xakc->xamc", inner_inverse, gathered, preferred_element_type=jnp.float32)
    flat = blocked.astype(jnp.float32)
    gate = jax.nn.sigmoid(flat * gate_gain + gate_bias)
    gated = (flat + gate * mixed).astype(jnp.bfloat16)
    full_rows = lax.all_to_all(
        gated.reshape(blocked.shape[0], tok_dev, ch_dev),
        "ch",
        split_axis=1,
        concat_axis=2,
        tiled=True,
    )
    rows_dev = full_rows.shape[1]
    width = full_rows.shape[2]
    rows_f = full_rows.astype(jnp.float32)
    scale = lax.rsqrt(jnp.mean(rows_f * rows_f, axis=-1, keepdims=True) + EPS)
    normed = (rows_f * scale * norm_gain).astype(jnp.bfloat16)
    normed_b = normed.reshape(seq_total * rows_dev, block_count, width_block)
    lifted = jnp.einsum(
        "rbi,bji->rbj",
        normed_b,
        lax.all_gather(up_weight, "seq", axis=1, tiled=True),
        preferred_element_type=jnp.float32,
    )
    hidden = jax.nn.gelu(lifted, approximate=True).astype(jnp.bfloat16)
    lowered = jnp.einsum(
        "rbj,bji->rbi",
        hidden,
        lax.all_gather(down_weight, "seq", axis=1, tiled=True),
        preferred_element_type=jnp.float32,
    )
    result_rows = (rows_f + lowered.reshape(seq_total, rows_dev, width)).astype(jnp.bfloat16)
    return lax.all_to_all(result_rows, "ch", split_axis=2, concat_axis=1, tiled=True)


def local(*args):
    tokens, up_weight = args[0], args[11]
    n = lax.axis_size("seq")
    if tokens.shape[2] % up_weight.shape[2] == 0 and n & (n - 1) == 0:
        return local_blocks(*args)
    return local_rows(*args)


def solution(mesh):
    in_specs = (
        P(None, "seq", "ch"),
        P(),
        P(),
        P("seq", None),
        P(None, "seq", "ch"),
        P(),
        P(),
        P(None, "seq"),
        P("ch"),
        P("ch"),
        P(),
        P(None, "seq", None),
        P(None, "seq", None),
    )
    out_specs = P(None, "seq", "ch")
    return jax.shard_map(local, mesh=mesh, in_specs=in_specs, out_specs=out_specs, check_vma=False)
```

```python
import functools

import jax
import jax.numpy as jnp
from jax import lax
from jax.experimental import pallas as pl
from jax.experimental.pallas import tpu as pltpu
from jax.sharding import PartitionSpec as P

VMEM_BYTES = 32 * 1024 * 1024
MOST_VMEM_BYTES = 56 * 1024 * 1024
GATE_VMEM_BYTES = 48 * 1024 * 1024
EPS = 1e-06
STEP_ROWS = 4
LAST_ROWS = 2


def params(size=VMEM_BYTES):
    return pltpu.CompilerParams(vmem_limit_bytes=size)


def first_kernel(tok_ref, w_ref, tw_ref, out_ref):
    n, step, rows, ch = out_ref.shape
    cols = tw_ref[...].T
    lane = lax.broadcasted_iota(jnp.int32, cols.shape, 1)
    for j in range(step):
        a = pl.program_id(0) * step + j
        res = jnp.dot(w_ref[...], tok_ref[0, j], preferred_element_type=jnp.float32)
        tw = jnp.sum(jnp.where(lane == a, cols, 0.0), axis=1, keepdims=True)
        out_ref[:, j] = (res * tw).astype(jnp.bfloat16).reshape(n, rows, ch)


def first_section(blocked, inner_forward, twiddle, s, n):
    _, a_dev, inner, ch = blocked.shape
    rows = inner // n
    step = STEP_ROWS if a_dev % STEP_ROWS == 0 else 1
    return pl.pallas_call(
        first_kernel,
        grid=(a_dev // step,),
        in_specs=[
            pl.BlockSpec((1, step, inner, ch), lambda a: (s, a, 0, 0)),
            pl.BlockSpec((inner, inner), lambda a: (0, 0)),
            pl.BlockSpec((a_dev, inner), lambda a: (0, 0)),
        ],
        out_specs=pl.BlockSpec((n, step, rows, ch), lambda a: (0, a, 0, 0)),
        out_shape=jax.ShapeDtypeStruct((n, a_dev, rows, ch), jnp.bfloat16),
        compiler_params=params(MOST_VMEM_BYTES),
        name="first_section",
    )(blocked, inner_forward, twiddle)


def outer_kernel(groups, fwd_ref, inv_ref, tw_ref, freq_ref, spread_ref, *rest):
    outs, (xs, fs, ys) = rest[:-3], rest[-3:]
    steps, outer, block = xs.shape
    xs[...] = jnp.swapaxes(spread_ref[...].astype(jnp.float32), 0, 1)
    fs[...] = jnp.swapaxes(freq_ref[...].astype(jnp.float32), 0, 1)
    tw = tw_ref[0]
    for k in range(steps):
        spectrum = jnp.dot(
            fwd_ref[...], xs[k].astype(jnp.bfloat16), preferred_element_type=jnp.float32
        )
        spectrum = (spectrum * fs[k]).astype(jnp.bfloat16)
        two = jnp.dot(inv_ref[...], spectrum, preferred_element_type=jnp.float32)
        ys[k] = two * tw[:, k : k + 1]
    res = jnp.swapaxes(ys[...], 0, 1).astype(jnp.bfloat16)
    n = outs[0].shape[0]
    res = res.reshape(n, outer // n, steps, block)
    first = 0
    for out, count in zip(outs, groups):
        out[...] = res[:, first : first + count]
        first += count


def outer_section(spread, forward, inverse, tw, freq, groups, n):
    outer, k_dev, ch = freq.shape
    rows, block = min(16, k_dev), min(256, ch)
    tw = tw.reshape(outer, k_dev // rows, rows).swapaxes(0, 1)
    return pl.pallas_call(
        functools.partial(outer_kernel, groups),
        grid=(k_dev // rows, ch // block),
        in_specs=[
            pl.BlockSpec((outer, outer), lambda h, c: (0, 0)),
            pl.BlockSpec((outer, outer), lambda h, c: (0, 0)),
            pl.BlockSpec((1, outer, rows), lambda h, c: (h, 0, 0)),
            pl.BlockSpec((outer, rows, block), lambda h, c: (0, h, c)),
            pl.BlockSpec((outer, rows, block), lambda h, c: (0, h, c)),
        ],
        out_specs=[
            pl.BlockSpec((n, count, rows, block), lambda h, c: (0, 0, h, c)) for count in groups
        ],
        out_shape=[
            jax.ShapeDtypeStruct((n, count, k_dev, ch), jnp.bfloat16) for count in groups
        ],
        scratch_shapes=[pltpu.VMEM((rows, outer, block), jnp.float32)] * 3,
        compiler_params=params(),
        name="outer_section",
    )(forward, inverse, tw, freq, spread)


def gate_kernel(tok_ref, w_ref, gain_ref, bias_ref, part_ref, gated_ref, sq_ref):
    flat = tok_ref[0, 0].astype(jnp.float32)
    section = part_ref[...].reshape(flat.shape)
    mixed = jnp.dot(w_ref[...], section, preferred_element_type=jnp.float32)
    gate = jax.nn.sigmoid(flat * gain_ref[...] + bias_ref[...])
    gated = (flat + gate * mixed).astype(jnp.bfloat16)
    gated_ref[0] = gated
    g = gated.astype(jnp.float32)
    sq = g * g
    part = sq[:, :128]
    for c in range(128, sq.shape[1], 128):
        part = part + sq[:, c : c + 128]
    sq_ref[0] = jnp.sum(part.T, axis=0, keepdims=True)


def gate_rows(blocked, inner_inverse, gain, bias, parts, s, first):
    _, _, inner, ch = blocked.shape
    n, count, rows, _ = parts.shape
    return pl.pallas_call(
        gate_kernel,
        grid=(count,),
        in_specs=[
            pl.BlockSpec((1, 1, inner, ch), lambda j: (s, first + j, 0, 0)),
            pl.BlockSpec((inner, inner), lambda j: (0, 0)),
            pl.BlockSpec((1, ch), lambda j: (0, 0)),
            pl.BlockSpec((1, ch), lambda j: (0, 0)),
            pl.BlockSpec((n, 1, rows, ch), lambda j: (0, j, 0, 0)),
        ],
        out_specs=[
            pl.BlockSpec((1, inner, ch), lambda j: (j, 0, 0)),
            pl.BlockSpec((1, 1, inner), lambda j: (j, 0, 0)),
        ],
        out_shape=[
            jax.ShapeDtypeStruct((count, inner, ch), jnp.bfloat16),
            jax.ShapeDtypeStruct((count, 1, inner), jnp.float32),
        ],
        compiler_params=params(GATE_VMEM_BYTES),
        name="gate_rows",
    )(blocked, inner_inverse, gain, bias, parts)


def mlp_kernel(width, n_sq, gated_ref, gain_ref, up_ref, down_ref, *rest):
    out_ref = rest[-1]
    blocks, _, wb = up_ref.shape
    total = rest[0][0]
    for sq_ref in rest[1:n_sq]:
        total = total + sq_ref[0]
    scale = lax.rsqrt(total * (1.0 / width) + EPS)
    scale = jnp.broadcast_to(scale, (128, scale.shape[1])).T[:, :1]
    for b in range(blocks):
        cols = slice(b * wb, (b + 1) * wb)
        g = gated_ref[0, :, cols].astype(jnp.float32)
        normed = (g * scale * gain_ref[:, cols]).astype(jnp.bfloat16)
        lifted = lax.dot_general(
            normed, up_ref[b], (((1,), (1,)), ((), ())), preferred_element_type=jnp.float32
        )
        hidden = jax.nn.gelu(lifted, approximate=True).astype(jnp.bfloat16)
        lowered = jnp.dot(hidden, down_ref[b], preferred_element_type=jnp.float32)
        out_ref[0, :, cols] = (g + lowered).astype(jnp.bfloat16)


def mlp_rows(gated, sqs, gain, weights, out, first, total, width):
    count, inner, ch = gated.shape
    specs = [
        pl.BlockSpec((1, inner, ch), lambda j: (j, 0, 0)),
        pl.BlockSpec((1, ch), lambda j: (0, 0)),
        pl.BlockSpec(memory_space=pltpu.VMEM),
        pl.BlockSpec(memory_space=pltpu.VMEM),
    ] + [pl.BlockSpec((1, 1, inner), lambda j: (j, 0, 0))] * len(sqs)
    args = [gated, gain, *weights, *sqs]
    aliases = {}
    if out is not None:
        aliases = {len(args): 0}
        specs.append(pl.BlockSpec(memory_space=pl.ANY))
        args.append(out)
    return pl.pallas_call(
        functools.partial(mlp_kernel, width, len(sqs)),
        grid=(count,),
        in_specs=specs,
        out_specs=pl.BlockSpec((1, inner, ch), lambda j: (first + j, 0, 0)),
        out_shape=jax.ShapeDtypeStruct((total, inner, ch), jnp.bfloat16),
        input_output_aliases=aliases,
        compiler_params=params(),
        name="mlp_rows",
    )(*args)


def after(x, *deps):
    return lax.optimization_barrier((x,) + deps)[0]


def exchange(x):
    return lax.all_to_all(x, "seq", split_axis=0, concat_axis=0, tiled=True)


def more_hidden(weights, n, step):
    pairs = [(j, j ^ step) for j in range(n)]
    got = [lax.ppermute(w, "seq", pairs) for w in weights]
    return [jnp.concatenate(both, axis=1) for both in zip(weights, got)], got


def local_blocks(
    tokens,
    inner_forward,
    outer_forward,
    twiddle_forward,
    freq_kernel,
    outer_inverse,
    inner_inverse,
    twiddle_inverse,
    gate_gain,
    gate_bias,
    norm_gain,
    up_weight,
    down_weight,
):
    seqs, tok_dev, ch = tokens.shape
    inner = inner_forward.shape[0]
    a_dev = tok_dev // inner
    n = lax.axis_size("seq")
    n_ch = lax.axis_size("ch")
    my_ch = lax.axis_index("ch")
    outer = n * a_dev
    blocked = tokens.reshape(seqs, a_dev, inner, ch)
    norm = lax.dynamic_slice_in_dim(norm_gain, my_ch * ch, ch, 0).reshape(1, ch)
    gain, bias = gate_gain.reshape(1, ch), gate_bias.reshape(1, ch)
    held = ch // up_weight.shape[2]
    weights = [
        lax.dynamic_slice_in_dim(w, my_ch * held, held, 0) for w in (up_weight, down_weight)
    ]
    weights, got = more_hidden(weights, n, n // 2)

    parts = [
        first_section(blocked, inner_forward, twiddle_forward, s, n) for s in range(seqs)
    ]
    step = n // 2
    spread = []
    waits = got
    for p in parts:
        last = exchange(after(p, *waits))
        spread.append(last.reshape(outer, -1, ch))
        if step > 1:
            step //= 2
            weights, got = more_hidden(weights, n, step)
        waits = [last, *got]
    out = None
    for s in range(seqs):
        last_rows = LAST_ROWS if s + 1 == seqs and a_dev > LAST_ROWS else 0
        groups = (a_dev - last_rows, last_rows) if last_rows else (a_dev,)
        back = outer_section(
            spread[s], outer_forward, outer_inverse, twiddle_inverse, freq_kernel, groups, n
        )
        first = 0
        for part, count in zip(back, groups):
            part = exchange(after(part, *waits))
            waits = [part] if out is None else [part, out]
            if out is not None:
                part = after(part, out)
            while step > 1:
                step //= 2
                weights, got = more_hidden(weights, n, step)
                waits += got
            gated, sq = gate_rows(blocked, inner_inverse, gain, bias, part, s, first)
            sqs = [sq] + [
                lax.ppermute(sq, "ch", [(j, (j + r) % n_ch) for j in range(n_ch)])
                for r in range(1, n_ch)
            ]
            out = mlp_rows(
                gated, sqs, norm, weights, out, s * a_dev + first, seqs * a_dev, ch * n_ch
            )
            first += count
    return out.reshape(seqs, tok_dev, ch)


def local_rows(
    tokens,
    inner_forward,
    outer_forward,
    twiddle_forward,
    freq_kernel,
    outer_inverse,
    inner_inverse,
    twiddle_inverse,
    gate_gain,
    gate_bias,
    norm_gain,
    up_weight,
    down_weight,
):
    seq_total, tok_dev, ch_dev = tokens.shape
    inner_size = inner_forward.shape[0]
    outer_dev = tok_dev // inner_size
    blocked = tokens.reshape(seq_total, outer_dev, inner_size, ch_dev)
    section_one = jnp.einsum(
        "kb,xabc->xakc", inner_forward, blocked, preferred_element_type=jnp.float32
    )
    section_one = (section_one * twiddle_forward[None, :, :, None]).astype(jnp.bfloat16)
    spread = lax.all_to_all(section_one, "seq", split_axis=2, concat_axis=1, tiled=True)
    spectrum = jnp.einsum(
        "ka,xabc->xkbc", outer_forward, spread, preferred_element_type=jnp.float32
    )
    spectrum = (spectrum * freq_kernel[None].astype(jnp.float32)).astype(jnp.bfloat16)
    section_two = jnp.einsum(
        "nk,xkbc->xnbc", outer_inverse, spectrum, preferred_element_type=jnp.float32
    )
    section_two = (section_two * twiddle_inverse[None, :, :, None]).astype(jnp.bfloat16)
    gathered = lax.all_to_all(section_two, "seq", split_axis=1, concat_axis=2, tiled=True)
    block_count = up_weight.shape[0]
    width_block = up_weight.shape[2]
    mixed = jnp.einsum("mk,xakc->xamc", inner_inverse, gathered, preferred_element_type=jnp.float32)
    flat = blocked.astype(jnp.float32)
    gate = jax.nn.sigmoid(flat * gate_gain + gate_bias)
    gated = (flat + gate * mixed).astype(jnp.bfloat16)
    full_rows = lax.all_to_all(
        gated.reshape(blocked.shape[0], tok_dev, ch_dev),
        "ch",
        split_axis=1,
        concat_axis=2,
        tiled=True,
    )
    rows_dev = full_rows.shape[1]
    width = full_rows.shape[2]
    rows_f = full_rows.astype(jnp.float32)
    scale = lax.rsqrt(jnp.mean(rows_f * rows_f, axis=-1, keepdims=True) + EPS)
    normed = (rows_f * scale * norm_gain).astype(jnp.bfloat16)
    normed_b = normed.reshape(seq_total * rows_dev, block_count, width_block)
    lifted = jnp.einsum(
        "rbi,bji->rbj",
        normed_b,
        lax.all_gather(up_weight, "seq", axis=1, tiled=True),
        preferred_element_type=jnp.float32,
    )
    hidden = jax.nn.gelu(lifted, approximate=True).astype(jnp.bfloat16)
    lowered = jnp.einsum(
        "rbj,bji->rbi",
        hidden,
        lax.all_gather(down_weight, "seq", axis=1, tiled=True),
        preferred_element_type=jnp.float32,
    )
    result_rows = (rows_f + lowered.reshape(seq_total, rows_dev, width)).astype(jnp.bfloat16)
    return lax.all_to_all(result_rows, "ch", split_axis=2, concat_axis=1, tiled=True)


def local(*args):
    tokens, up_weight = args[0], args[11]
    n = lax.axis_size("seq")
    if tokens.shape[2] % up_weight.shape[2] == 0 and n & (n - 1) == 0:
        return local_blocks(*args)
    return local_rows(*args)


def solution(mesh):
    in_specs = (
        P(None, "seq", "ch"),
        P(),
        P(),
        P("seq", None),
        P(None, "seq", "ch"),
        P(),
        P(),
        P(None, "seq"),
        P("ch"),
        P("ch"),
        P(),
        P(None, "seq", None),
        P(None, "seq", None),
    )
    out_specs = P(None, "seq", "ch")
    return jax.shard_map(local, mesh=mesh, in_specs=in_specs, out_specs=out_specs, check_vma=False)
```
